32 devices in a mesh: tbl: 16 (over z, y, x), row: 2 (over core).
Axes of the slice: x: 2, y: 2, z: 4, core: 2. Of those that a mesh axis runs over, the one named last changes fastest.
Arguments:
- slab: bfloat16 [2048, 256], P(('tbl', 'row')), may hold values from -1.1953125 to 1.1953125
- counts: int32 [4096, 2048], P(None, ('tbl', 'row')), may hold values 0 or 1
- cross_down: bfloat16 [4096, 512], replicated, may hold values from -0.09375 to 0.09375
- cross_up: bfloat16 [512, 4096], replicated, may hold values from -0.25 to 0.25
- cross_bias: float32 [4096], replicated, may hold values from -3 to 3
- out_weight: float32 [4096], replicated, may hold values from -0.09375 to 0.09375
- labels: int32 [4096], P(('tbl', 'row')), may hold values 0 or 1
Outputs:
- grad_slab: float32 [2048, 256], P(('tbl', 'row'))
- grad_down: bfloat16 [4096, 512], P(('tbl', 'row'))
- grad_up: bfloat16 [512, 4096], P(None, ('tbl', 'row'))
- grad_bias: float32 [4096], P(('tbl', 'row'))
- grad_out: float32 [4096], P(('tbl', 'row'))
The draws below stay inside these ranges and needn't reach their ends.
All inputs are finite; a program needn't handle non-finite values. No bound on the sum of `counts` or of `labels` on one device may be relied on, other than what follows from the above.
Results may differ from the reference program's by a relative error of at most 0.022.
Values may be sent and summed in bfloat16 or wider, within the bound.
A program may use at most 128 MiB of HBM per device.

```python
import jax
import jax.numpy as jnp
from jax import lax

EMBED = 256
TABLES = 16
RANK = 512
ROWS_DEV = 64
CROSS = 4096
BATCH = 4096
TOTAL_ROWS = 2048
N_TBL = 16
N_ROW = 2


def set_ends(drawn, own_key, smallest, largest):
    index_at = [jax.random.randint(jax.random.fold_in(own_key, axis), (), 0, length) for axis, length in enumerate(drawn.shape)]
    widest = drawn.shape.index(max(drawn.shape))
    next_to = index_at[:widest] + [(index_at[widest] + 1) % drawn.shape[widest]] + index_at[widest + 1:]
    return drawn.at[tuple(index_at)].set(smallest).at[tuple(next_to)].set(largest)


def steps_of(own_key, extent, cuts, smallest, top_value):
    loudness, own = 1.0, jax.random.fold_in(own_key, 6)
    for position, blocks in cuts:
        draws = jnp.exp(jax.random.uniform(jax.random.fold_in(own, position), (blocks,), jnp.float32, smallest / len(cuts), top_value / len(cuts)))
        loudness = loudness * jnp.repeat(draws, extent[position] // blocks).reshape([-1 if axis == position else 1 for axis in range(len(extent))])
    return loudness


def normal_values(stream_key, dims, deviation, limit, shards=(), held_as=jnp.bfloat16):
    result = deviation * jax.random.normal(stream_key, dims, jnp.float32)
    if shards:
        result = result * steps_of(stream_key, dims, shards, -0.22, 0.18)
    return jnp.clip(result, -limit, limit).astype(held_as)


def setup_inputs(seed: int = 0) -> dict:
    streams_of = jax.random.split(jax.random.key(seed), 8)
    slab = normal_values(streams_of[0], (TOTAL_ROWS, EMBED), 0.18, 1.1953125, ((0, 32),))
    counts = set_ends((jax.random.randint(streams_of[1], (BATCH, TOTAL_ROWS), 0, 32) < 1).astype(jnp.int32), jax.random.fold_in(streams_of[1], 1), 0, 1)
    cross_down = normal_values(streams_of[2], (CROSS, RANK), CROSS ** -0.5, 0.09375)
    cross_up = normal_values(streams_of[3], (RANK, CROSS), RANK ** -0.5, 0.25)
    cross_bias = normal_values(streams_of[4], (CROSS,), 0.5, 3.0, (), jnp.float32)
    out_weight = normal_values(streams_of[5], (CROSS,), CROSS ** -0.5, 0.09375, (), jnp.float32)
    labels = set_ends((jax.random.randint(streams_of[6], (BATCH,), 0, 2) < 1).astype(jnp.int32), jax.random.fold_in(streams_of[6], 1), 0, 1)
    return {"slab": slab, "counts": counts, "cross_down": cross_down, "cross_up": cross_up, "cross_bias": cross_bias, "out_weight": out_weight, "labels": labels}


def reference(slab, counts, cross_down, cross_up, cross_bias, out_weight, labels):
    per_group = TABLES // N_TBL
    row_span = N_ROW // per_group
    group_rows = ROWS_DEV * N_ROW
    owner_table = ((jnp.arange(N_ROW, dtype=jnp.int32) // row_span)[:, None] == jnp.arange(per_group, dtype=jnp.int32)[None, :]).astype(jnp.float32)

    def pool_group(group):
        start_row = (group * group_rows).astype(jnp.int32)
        counted = lax.dynamic_slice_in_dim(counts, start_row, group_rows, 1).astype(jnp.float32).reshape(BATCH, N_ROW, ROWS_DEV)
        slab_rows = lax.dynamic_slice_in_dim(slab, start_row, group_rows, 0).astype(jnp.float32).reshape(N_ROW, ROWS_DEV, EMBED)
        partial_value = jnp.einsum("bkr,kre->kbe", counted, slab_rows).astype(jnp.bfloat16)
        partial_value = lax.optimization_barrier(partial_value).astype(jnp.float32)
        return jnp.einsum("kbe,kt->bte", partial_value, owner_table).reshape(BATCH, per_group * EMBED)

    stacked = lax.map(pool_group, jnp.arange(N_TBL, dtype=jnp.int32))
    pooled = stacked.transpose(1, 0, 2).reshape(BATCH, CROSS).astype(jnp.bfloat16)
    pooled_full = pooled.astype(jnp.float32)
    squeezed = jnp.dot(pooled, cross_down, preferred_element_type=jnp.float32).astype(jnp.bfloat16)
    cross_gain = jnp.dot(squeezed, cross_up, preferred_element_type=jnp.float32) + cross_bias
    crossed = pooled_full * cross_gain + pooled_full
    logits = jnp.sum(crossed * out_weight, axis=1)
    grad_logits = jax.nn.sigmoid(logits) - labels.astype(jnp.float32)
    grad_out = jnp.sum(crossed * grad_logits[:, None], axis=0)
    grad_crossed = grad_logits[:, None] * out_weight
    grad_gain = grad_crossed * pooled_full
    grad_bias = jnp.sum(grad_gain, axis=0)
    gain_half = grad_gain.astype(jnp.bfloat16)
    grad_up = jnp.dot(squeezed.T, gain_half, preferred_element_type=jnp.float32).astype(jnp.bfloat16)
    grad_squeezed = jnp.dot(gain_half, cross_up.T, preferred_element_type=jnp.float32).astype(jnp.bfloat16)
    grad_down = jnp.dot(pooled.T, grad_squeezed, preferred_element_type=jnp.float32).astype(jnp.bfloat16)
    grad_pooled = (grad_crossed * (cross_gain + 1.0) + jnp.dot(grad_squeezed, cross_down.T, preferred_element_type=jnp.float32)).astype(jnp.bfloat16)

    def back_group(group):
        start_row = (group * group_rows).astype(jnp.int32)
        counted = lax.dynamic_slice_in_dim(counts, start_row, group_rows, 1).astype(jnp.float32).reshape(BATCH, N_ROW, ROWS_DEV)
        columns = lax.dynamic_slice_in_dim(grad_pooled, (group * per_group * EMBED).astype(jnp.int32), per_group * EMBED, 1).astype(jnp.float32).reshape(BATCH, per_group, EMBED)
        selected = jnp.einsum("bte,kt->kbe", columns, owner_table)
        return jnp.einsum("bkr,kbe->kre", counted, selected).reshape(group_rows, EMBED)

    grad_slab = lax.map(back_group, jnp.arange(N_TBL, dtype=jnp.int32)).reshape(TOTAL_ROWS, EMBED)
    return grad_slab, grad_down, grad_up, grad_bias, grad_out
```

```python
import functools
import math

import jax
import jax.numpy as jnp
from jax import lax
from jax.sharding import Mesh, PartitionSpec as P


def inner_count(count):
    width = max(1, math.isqrt(count))
    while count % width:
        width -= 1
    return width


def local(slab, counts, cross_down, cross_up, cross_bias, out_weight, labels):
    z_count, q_count, row_count = (lax.axis_size(name) for name in ("z", "q", "row"))
    table_count = z_count * q_count
    rows_local, embed = slab.shape
    samples = labels.shape[0]
    rank = cross_down.shape[1]
    half, full = jnp.bfloat16, jnp.float32
    dot = functools.partial(jnp.einsum, preferred_element_type=full)
    my_table = lax.axis_index("z") * q_count + lax.axis_index("q")
    flipped = counts.T.astype(half).reshape(rows_local, z_count, q_count, row_count, samples)
    flipped = flipped.transpose(1, 3, 0, 2, 4).reshape(z_count * row_count, rows_local, q_count * samples)
    mine = lax.all_to_all(flipped, ("z", "row"), 0, 0, tiled=True)
    mine = mine.reshape(z_count * row_count * rows_local, q_count, samples)
    own = lax.all_to_all(mine, "q", 1, 0, tiled=True)
    own = own.reshape(q_count, z_count, row_count * rows_local, samples).swapaxes(0, 1)
    tables = lax.all_gather(slab, ("z", "q", "row"), axis=0, tiled=True)
    tables = tables.reshape(table_count, row_count * rows_local, embed)
    weighted = (tables.astype(full) * out_weight.reshape(table_count, 1, embed)).astype(half)
    down = cross_down.reshape(table_count, embed, rank)
    up = cross_up.reshape(rank, table_count, embed)
    factors = jnp.concatenate(
        [dot("tpe,ter->tpr", tables, down), dot("tpe,rte->tpr", weighted, up)], axis=2
    ).astype(half)
    head = ((1.0 + cross_bias) * out_weight).reshape(table_count, 1, embed)
    direct = jnp.sum(tables.astype(full) * head, axis=2)
    own = own.reshape(table_count * row_count * rows_local, samples)
    both = dot("ps,pr->sr", own, factors.reshape(-1, 2 * rank))
    logits = jnp.sum(own.astype(full) * direct.reshape(-1, 1), axis=0)
    logits = logits + jnp.sum(both[:, :rank] * both[:, rank:], axis=1)
    grad = jax.nn.sigmoid(logits) - labels.astype(full)
    tail = jnp.zeros((samples, 128), full).at[:, 0].set(grad)
    scaled = jnp.concatenate([both * grad[:, None], tail], axis=1).astype(half)
    scaled = lax.all_gather(scaled, "q", axis=0, tiled=True)
    partial = dot("ps,sr->pr", mine.reshape(-1, q_count * samples), scaled).astype(half)
    partial = partial.reshape(z_count * row_count, rows_local, 2 * rank + 128)
    summed = lax.all_to_all(partial, ("z", "row"), 0, 0, tiled=True)
    summed = jnp.sum(summed.astype(full), axis=0)
    whole = lax.all_gather(summed.astype(half), "row", axis=0, tiled=True)
    start = my_table * embed
    down_own = lax.dynamic_slice_in_dim(cross_down, start, embed, 0)
    up_own = lax.dynamic_slice_in_dim(cross_up, start, embed, 1)
    weight_own = lax.dynamic_slice_in_dim(out_weight, start, embed, 0)
    bias_own = lax.dynamic_slice_in_dim(cross_bias, start, embed, 0)
    left, right, count_sum = summed[:, :rank], summed[:, rank : 2 * rank], summed[:, 2 * rank :][:, :1]
    grad_slab = (
        (1.0 + bias_own) * weight_own * count_sum
        + weight_own * dot("pr,re->pe", left.astype(half), up_own)
        + dot("pr,er->pe", right.astype(half), down_own)
    )
    columns = embed // row_count
    at = lax.axis_index("row") * columns
    slab_table = lax.dynamic_index_in_dim(tables, my_table, 0, False)
    slab_own = lax.dynamic_slice_in_dim(slab_table, at, columns, 1)
    weight_part = lax.dynamic_slice_in_dim(weight_own, at, columns, 0)
    bias_part = lax.dynamic_slice_in_dim(bias_own, at, columns, 0)
    up_part = lax.dynamic_slice_in_dim(up_own, at, columns, 1)
    grad_down = dot("pe,pr->er", slab_own, whole[:, rank : 2 * rank])
    core = dot("pr,pe->re", whole[:, :rank], slab_own)
    total = dot("pe,pr->er", slab_own, whole[:, 2 * rank :])[:, 0]
    grad_bias = weight_part * total
    grad_out = (1.0 + bias_part) * total + jnp.sum(up_part.astype(full) * core, axis=0)
    return (
        grad_slab,
        grad_down.astype(half),
        (core * weight_part).astype(half),
        grad_bias,
        grad_out,
    )


def solution(mesh):
    tbl_count, row_count = mesh.shape["tbl"], mesh.shape["row"]
    q_count = inner_count(tbl_count)
    finer = Mesh(mesh.devices.reshape(tbl_count // q_count, q_count, row_count), ("z", "q", "row"))
    every = ("z", "q", "row")
    placed = (P(every, None), P(None, every), P(), P(), P(), P(), P(every))
    return jax.shard_map(
        local,
        mesh=finer,
        in_specs=placed,
        out_specs=(P(every, None), P(every, None), P(None, every), P(every), P(every)),
        check_vma=False,
    )
```

```python
import functools
import math

import jax
import jax.numpy as jnp
from jax import lax
from jax.experimental import pallas as pl
from jax.experimental.pallas import tpu as pltpu
from jax.sharding import Mesh, PartitionSpec as P


def inner_count(count):
    width = max(1, math.isqrt(count))
    while count % width:
        width -= 1
    return width


def kernel(
    slab, flipped, down_hbm, up_hbm, bias, weight, labels,
    sum_out, whole_out, slab_out,
    down, up, send_counts, mine, own, slabs, factors, scaled, part_send, parts, whole,
    load_sem, count_send, count_recv, own_send, own_recv,
    slab_z_send, slab_z_recv, slab_q_send, slab_q_recv, slab_r_send, slab_r_recv,
    scaled_send, scaled_recv, part_send_sem, part_recv_sem, whole_send, whole_recv,
):
    z_count, q_count, row_count = (lax.axis_size(name) for name in ("z", "q", "row"))
    z, q, c = (lax.axis_index(name) for name in ("z", "q", "row"))
    rows, embed = slab.shape
    samples = labels.shape[0]
    rank = down.shape[1]
    half, full = jnp.bfloat16, jnp.float32
    group = z * row_count + c

    def device(at_z, at_q, at_c):
        return (at_z, at_q, at_c)

    def remote(source, target, send, recv, to):
        return pltpu.make_async_remote_copy(
            src_ref=source, dst_ref=target, send_sem=send, recv_sem=recv,
            device_id=to, device_id_type=pl.DeviceIdType.MESH,
        )

    z_peers = [lax.rem(z + step, z_count) for step in range(1, z_count)]
    q_peers = [lax.rem(q + step, q_count) for step in range(1, q_count)]
    c_peers = [lax.rem(c + step, row_count) for step in range(1, row_count)]
    group_peers = [(z, at_c) for at_c in c_peers]
    for at_z in z_peers:
        group_peers += [(at_z, at_c) for at_c in [c] + c_peers]

    loads = [
        pltpu.make_async_copy(down_hbm, down, load_sem.at[0]),
        pltpu.make_async_copy(up_hbm, up, load_sem.at[1]),
    ]
    for load in loads:
        load.start()
    barrier = pltpu.get_barrier_semaphore()
    for at_z, at_c in group_peers:
        pl.semaphore_signal(barrier, inc=1, device_id=device(at_z, q, at_c), device_id_type=pl.DeviceIdType.MESH)
    for at_q in q_peers:
        pl.semaphore_signal(barrier, inc=1, device_id=device(z, at_q, c), device_id_type=pl.DeviceIdType.MESH)
    slabs[q, z, c] = slab[...]

    def fill(at_z, at_c):
        for at_q in range(q_count):
            start = pl.multiple_of(((at_z * q_count + at_q) * row_count + at_c) * samples, 128)
            block = flipped[:, pl.ds(start, samples)].astype(half)
            if at_z is z and at_c is c:
                mine[group, :, at_q * samples : (at_q + 1) * samples] = block
            else:
                send_counts[at_z * row_count + at_c, :, at_q * samples : (at_q + 1) * samples] = block

    for at_z, at_c in group_peers:
        fill(at_z, at_c)
    pl.semaphore_wait(barrier, len(group_peers) + len(q_peers))

    sends = []
    for at_z in z_peers:
        sends.append(remote(slabs.at[q, z, c], slabs.at[q, z, c], slab_z_send.at[at_z], slab_z_recv.at[z], device(at_z, q, c)))
        sends[-1].start()
    for at_z, at_c in group_peers:
        to = at_z * row_count + at_c
        sends.append(remote(send_counts.at[to], mine.at[group], count_send.at[to], count_recv.at[group], device(at_z, q, at_c)))
        sends[-1].start()
    fill(z, c)

    def forward_counts(index):
        for at_q in q_peers:
            block = mine.at[index, :, pl.ds(pl.multiple_of(at_q * samples, 128), samples)]
            remote(block, own.at[q, index], own_send.at[at_q], own_recv.at[q], device(z, at_q, c)).start()

    forward_counts(group)
    for at_z in z_peers:
        remote(slabs.at[q, at_z, c], slabs.at[q, at_z, c], slab_z_send.at[at_z], slab_z_recv.at[at_z], device(at_z, q, c)).wait_recv()
    for at_q in q_peers:
        sends.append(remote(slabs.at[q, :, c], slabs.at[q, :, c], slab_q_send.at[at_q], slab_q_recv.at[q], device(z, at_q, c)))
        sends[-1].start()
    for at_c in c_peers:
        remote(slabs.at[q, :, c], slabs.at[q, :, c], slab_r_send.at[at_c], slab_r_recv.at[c], device(z, q, at_c)).start()
    for at_q in q_peers:
        remote(slabs.at[at_q, :, c], slabs.at[at_q, :, c], slab_q_send.at[at_q], slab_q_recv.at[at_q], device(z, at_q, c)).wait_recv()
        for at_c in c_peers:
            remote(slabs.at[at_q, :, c], slabs.at[at_q, :, c], slab_r_send.at[at_c], slab_r_recv.at[c], device(z, q, at_c)).start()
    for at_c in c_peers:
        remote(slabs.at[:, :, at_c], slabs.at[:, :, at_c], slab_r_send.at[at_c], slab_r_recv.at[at_c], device(z, q, at_c)).wait_recv()

    for at_z, at_c in group_peers:
        index = at_z * row_count + at_c
        remote(mine.at[index], mine.at[index], count_send.at[index], count_recv.at[index], device(at_z, q, at_c)).wait_recv()
        forward_counts(index)

    for load in loads:
        load.wait()

    def one_table(table, carry):
        at = pl.multiple_of(table * embed, 128)
        at_z, at_q = table // q_count, lax.rem(table, q_count)
        block = slabs[at_q, at_z].reshape(row_count * rows, embed)
        wide = block.astype(full)
        heavy = weight[:, pl.ds(at, embed)]
        factors[at_q, at_z, :, :rank] = jnp.dot(block, down[pl.ds(at, embed), :], preferred_element_type=full).astype(half)
        factors[at_q, at_z, :, rank : 2 * rank] = lax.dot_general(
            (wide * heavy).astype(half), up[:, pl.ds(at, embed)], (((1,), (1,)), ((), ())), preferred_element_type=full
        ).astype(half)
        direct = jnp.sum(wide * (heavy * (1.0 + bias[:, pl.ds(at, embed)])), axis=1, keepdims=True)
        upper = direct.astype(half).astype(full)
        lane = lax.broadcasted_iota(jnp.int32, (row_count * rows, 128), 1)
        both = jnp.where(lane == 0, upper, jnp.where(lane == 1, direct - upper, 0.0))
        factors[at_q, at_z, :, 2 * rank :] = both.astype(half)
        return carry

    lax.fori_loop(0, z_count * q_count, one_table, 0)

    own[q] = mine[:, :, pl.ds(pl.multiple_of(q * samples, 128), samples)]
    total = None
    for at_q in [q] + q_peers:
        if at_q is not q:
            remote(own.at[at_q], own.at[at_q], own_send.at[at_q], own_recv.at[at_q], device(z, at_q, c)).wait_recv()
        term = lax.dot_general(
            own[at_q].reshape(z_count * row_count * rows, samples),
            factors[at_q].reshape(z_count * row_count * rows, 2 * rank + 128),
            (((0,), (0,)), ((), ())), preferred_element_type=full,
        )
        total = term if total is None else total + term
    logits = jnp.sum(total[:, 2 * rank :], axis=1, keepdims=True)
    logits = logits + jnp.sum(total[:, :rank] * total[:, rank : 2 * rank], axis=1, keepdims=True)
    grad = jax.nn.sigmoid(logits) - labels[...].astype(full)
    scaled[q, :, : 2 * rank] = (total[:, : 2 * rank] * grad).astype(half)
    lane = lax.broadcasted_iota(jnp.int32, (samples, 128), 1)
    scaled[q, :, 2 * rank :] = jnp.where(lane == 0, grad, 0.0).astype(half)
    for at_q in q_peers:
        sends.append(remote(scaled.at[q], scaled.at[q], scaled_send.at[at_q], scaled_recv.at[q], device(z, at_q, c)))
        sends[-1].start()
    for at_q in q_peers:
        remote(scaled.at[at_q], scaled.at[at_q], scaled_send.at[at_q], scaled_recv.at[at_q], device(z, at_q, c)).wait_recv()
    gathered = scaled[...].reshape(q_count * samples, 2 * rank + 128)
    for at_z in z_peers + [z]:
        counted = mine[pl.ds(at_z * row_count, row_count)].reshape(row_count * rows, q_count * samples)
        term = jnp.dot(counted, gathered, preferred_element_type=full).astype(half)
        part_send[pl.ds(at_z * row_count, row_count)] = term.reshape(row_count, rows, 2 * rank + 128)
        for at_c in [c] + c_peers:
            if at_z is z and at_c is c:
                continue
            to = at_z * row_count + at_c
            sends.append(remote(part_send.at[to], parts.at[group], part_send_sem.at[to], part_recv_sem.at[group], device(at_z, q, at_c)))
            sends[-1].start()
    summed = part_send[group].astype(full)
    for at_z, at_c in group_peers:
        index = at_z * row_count + at_c
        remote(parts.at[index], parts.at[index], part_send_sem.at[index], part_recv_sem.at[index], device(at_z, q, at_c)).wait_recv()
        summed = summed + parts[index].astype(full)
    whole[c] = summed.astype(half)
    for at_c in c_peers:
        sends.append(remote(whole.at[c], whole.at[c], whole_send.at[at_c], whole_recv.at[c], device(z, q, at_c)))
        sends[-1].start()
    sum_out[...] = summed
    slab_out[...] = slabs[q, z].reshape(row_count * rows, embed)
    for at_c in c_peers:
        remote(whole.at[at_c], whole.at[at_c], whole_send.at[at_c], whole_recv.at[at_c], device(z, q, at_c)).wait_recv()
    whole_out[...] = whole[...].reshape(row_count * rows, 2 * rank + 128)
    for copy in sends:
        copy.wait_send()
    for at_q in q_peers:
        remote(own.at[at_q], own.at[at_q], own_send.at[at_q], own_recv.at[at_q], device(z, at_q, c)).wait_send()
    for at_c in c_peers:
        remote(slabs.at[:, :, at_c], slabs.at[:, :, at_c], slab_r_send.at[at_c], slab_r_recv.at[at_c], device(z, q, at_c)).wait_send()


def local(slab, counts, cross_down, cross_up, cross_bias, out_weight, labels):
    z_count, q_count, row_count = (lax.axis_size(name) for name in ("z", "q", "row"))
    rows, embed = slab.shape
    samples = labels.shape[0]
    rank, width = cross_down.shape[1], cross_down.shape[0]
    half, full = jnp.bfloat16, jnp.float32
    dot = functools.partial(jnp.einsum, preferred_element_type=full)
    groups, table_rows, wide = z_count * row_count, row_count * rows, 2 * rank + 128
    vmem, anywhere = pl.BlockSpec(memory_space=pltpu.VMEM), pl.BlockSpec(memory_space=pl.ANY)
    sem = pltpu.SemaphoreType.DMA
    summed, whole, slab_table = pl.pallas_call(
        kernel,
        out_shape=(
            jax.ShapeDtypeStruct((rows, wide), full),
            jax.ShapeDtypeStruct((table_rows, wide), half),
            jax.ShapeDtypeStruct((table_rows, embed), half),
        ),
        in_specs=[vmem, vmem, anywhere, anywhere, vmem, vmem, vmem],
        out_specs=(vmem, vmem, vmem),
        scratch_shapes=[
            pltpu.VMEM((width, rank), half),
            pltpu.VMEM((rank, width), half),
            pltpu.VMEM((groups, rows, q_count * samples), half),
            pltpu.VMEM((groups, rows, q_count * samples), half),
            pltpu.VMEM((q_count, groups, rows, samples), half),
            pltpu.VMEM((q_count, z_count, row_count, rows, embed), half),
            pltpu.VMEM((q_count, z_count, table_rows, wide), half),
            pltpu.VMEM((q_count, samples, wide), half),
            pltpu.VMEM((groups, rows, wide), half),
            pltpu.VMEM((groups, rows, wide), half),
            pltpu.VMEM((row_count, rows, wide), half),
            sem((2,)),
            sem((groups,)), sem((groups,)), sem((q_count,)), sem((q_count,)),
            sem((z_count,)), sem((z_count,)), sem((q_count,)), sem((q_count,)), sem((row_count,)), sem((row_count,)),
            sem((q_count,)), sem((q_count,)), sem((groups,)), sem((groups,)), sem((row_count,)), sem((row_count,)),
        ],
        compiler_params=pltpu.CompilerParams(collective_id=0, has_side_effects=True, vmem_limit_bytes=60 * 2**20),
    )(slab, counts.T, cross_down, cross_up, cross_bias.reshape(1, -1), out_weight.reshape(1, -1), labels.reshape(-1, 1))
    my_table = lax.axis_index("z") * q_count + lax.axis_index("q")
    start = my_table * embed
    down_own = lax.dynamic_slice_in_dim(cross_down, start, embed, 0)
    up_own = lax.dynamic_slice_in_dim(cross_up, start, embed, 1)
    weight_own = lax.dynamic_slice_in_dim(out_weight, start, embed, 0)
    bias_own = lax.dynamic_slice_in_dim(cross_bias, start, embed, 0)
    left, right, count_sum = summed[:, :rank], summed[:, rank : 2 * rank], summed[:, 2 * rank :][:, :1]
    grad_slab = (
        (1.0 + bias_own) * weight_own * count_sum
        + weight_own * dot("pr,re->pe", left.astype(half), up_own)
        + dot("pr,er->pe", right.astype(half), down_own)
    )
    columns = embed // row_count
    at = lax.axis_index("row") * columns
    slab_own = lax.dynamic_slice_in_dim(slab_table, at, columns, 1)
    weight_part = lax.dynamic_slice_in_dim(weight_own, at, columns, 0)
    bias_part = lax.dynamic_slice_in_dim(bias_own, at, columns, 0)
    up_part = lax.dynamic_slice_in_dim(up_own, at, columns, 1)
    grad_down = dot("pe,pr->er", slab_own, whole[:, rank : 2 * rank])
    core = dot("pr,pe->re", whole[:, :rank], slab_own)
    total = dot("pe,pr->er", slab_own, whole[:, 2 * rank :])[:, 0]
    grad_bias = weight_part * total
    grad_out = (1.0 + bias_part) * total + jnp.sum(up_part.astype(full) * core, axis=0)
    return (
        grad_slab,
        grad_down.astype(half),
        (core * weight_part).astype(half),
        grad_bias,
        grad_out,
    )


def solution(mesh):
    tbl_count, row_count = mesh.shape["tbl"], mesh.shape["row"]
    q_count = inner_count(tbl_count)
    finer = Mesh(mesh.devices.reshape(tbl_count // q_count, q_count, row_count), ("z", "q", "row"))
    every = ("z", "q", "row")
    placed = (P(every, None), P(None, every), P(), P(), P(), P(), P(every))
    return jax.shard_map(
        local,
        mesh=finer,
        in_specs=placed,
        out_specs=(P(every, None), P(every, None), P(None, every), P(every), P(every)),
        check_vma=False,
    )
```

```python
import functools
import math

import jax
import jax.numpy as jnp
from jax import lax
from jax.experimental import pallas as pl
from jax.experimental.pallas import tpu as pltpu
from jax.sharding import Mesh, PartitionSpec as P


def inner_count(count):
    width = max(1, math.isqrt(count))
    while count % width:
        width -= 1
    return width


def kernel(
    inside, out_count, slab, flipped, down_hbm, up_hbm, bias, weight, labels,
    *refs,
):
    outs, rest = refs[:out_count], refs[out_count:]
    (
    down, up, send_counts, mine, own, slabs, factors, scaled, part_send, parts, whole,
    load_sem, count_send, count_recv, own_send, own_recv,
    slab_z_send, slab_z_recv, slab_q_send, slab_q_recv, slab_r_send, slab_r_recv,
    scaled_send, scaled_recv, part_send_sem, part_recv_sem, whole_send, whole_recv,
    ) = rest
    z_count, q_count, row_count = (lax.axis_size(name) for name in ("z", "q", "row"))
    z, q, c = (lax.axis_index(name) for name in ("z", "q", "row"))
    rows, embed = slab.shape
    samples = labels.shape[1]
    rank = down.shape[1]
    half, full = jnp.bfloat16, jnp.float32
    group = z * row_count + c

    def device(at_z, at_q, at_c):
        return (at_z, at_q, at_c)

    def remote(source, target, send, recv, to):
        return pltpu.make_async_remote_copy(
            src_ref=source, dst_ref=target, send_sem=send, recv_sem=recv,
            device_id=to, device_id_type=pl.DeviceIdType.MESH,
        )

    z_peers = [lax.rem(z + step, z_count) for step in range(1, z_count)]
    q_peers = [lax.rem(q + step, q_count) for step in range(1, q_count)]
    c_peers = [lax.rem(c + step, row_count) for step in range(1, row_count)]
    group_peers = [(z, at_c) for at_c in c_peers]
    for at_z in z_peers:
        group_peers += [(at_z, at_c) for at_c in [c] + c_peers]

    loads = [
        pltpu.make_async_copy(down_hbm, down, load_sem.at[0]),
        pltpu.make_async_copy(up_hbm, up, load_sem.at[1]),
    ]
    for load in loads:
        load.start()
    barrier = pltpu.get_barrier_semaphore()
    for at_z, at_c in group_peers:
        pl.semaphore_signal(barrier, inc=1, device_id=device(at_z, q, at_c), device_id_type=pl.DeviceIdType.MESH)
    for at_q in q_peers:
        pl.semaphore_signal(barrier, inc=1, device_id=device(z, at_q, c), device_id_type=pl.DeviceIdType.MESH)
    slabs[q, z, c] = slab[...]

    def fill(at_z, at_c):
        for at_q in range(q_count):
            start = pl.multiple_of(((at_z * q_count + at_q) * row_count + at_c) * samples, 128)
            block = flipped[:, pl.ds(start, samples)].astype(half)
            if at_z is z and at_c is c:
                mine[group, :, at_q * samples : (at_q + 1) * samples] = block
            else:
                send_counts[at_z * row_count + at_c, :, at_q * samples : (at_q + 1) * samples] = block

    for at_z, at_c in group_peers:
        fill(at_z, at_c)
    pl.semaphore_wait(barrier, len(group_peers) + len(q_peers))

    sends = []
    for at_z in z_peers:
        sends.append(remote(slabs.at[q, z, c], slabs.at[q, z, c], slab_z_send.at[at_z], slab_z_recv.at[z], device(at_z, q, c)))
        sends[-1].start()
    for at_z, at_c in group_peers:
        to = at_z * row_count + at_c
        sends.append(remote(send_counts.at[to], mine.at[group], count_send.at[to], count_recv.at[group], device(at_z, q, at_c)))
        sends[-1].start()
    fill(z, c)

    def forward_counts(index):
        for at_q in q_peers:
            block = mine.at[index, :, pl.ds(pl.multiple_of(at_q * samples, 128), samples)]
            remote(block, own.at[q, index], own_send.at[at_q], own_recv.at[q], device(z, at_q, c)).start()

    forward_counts(group)
    for at_z in z_peers:
        remote(slabs.at[q, at_z, c], slabs.at[q, at_z, c], slab_z_send.at[at_z], slab_z_recv.at[at_z], device(at_z, q, c)).wait_recv()
    for at_q in q_peers:
        sends.append(remote(slabs.at[q, :, c], slabs.at[q, :, c], slab_q_send.at[at_q], slab_q_recv.at[q], device(z, at_q, c)))
        sends[-1].start()
    for at_c in c_peers:
        remote(slabs.at[q, :, c], slabs.at[q, :, c], slab_r_send.at[at_c], slab_r_recv.at[c], device(z, q, at_c)).start()
    for at_q in q_peers:
        remote(slabs.at[at_q, :, c], slabs.at[at_q, :, c], slab_q_send.at[at_q], slab_q_recv.at[at_q], device(z, at_q, c)).wait_recv()
        for at_c in c_peers:
            remote(slabs.at[at_q, :, c], slabs.at[at_q, :, c], slab_r_send.at[at_c], slab_r_recv.at[c], device(z, q, at_c)).start()
    for at_c in c_peers:
        remote(slabs.at[:, :, at_c], slabs.at[:, :, at_c], slab_r_send.at[at_c], slab_r_recv.at[at_c], device(z, q, at_c)).wait_recv()

    for at_z, at_c in group_peers:
        index = at_z * row_count + at_c
        remote(mine.at[index], mine.at[index], count_send.at[index], count_recv.at[index], device(at_z, q, at_c)).wait_recv()
        forward_counts(index)

    for load in loads:
        load.wait()

    def one_table(table, carry):
        at = pl.multiple_of(table * embed, 128)
        at_z, at_q = table // q_count, lax.rem(table, q_count)
        block = slabs[at_q, at_z].reshape(row_count * rows, embed)
        wide = block.astype(full)
        heavy = weight[:, pl.ds(at, embed)]
        factors[at_q, at_z, :, :rank] = jnp.dot(block, down[pl.ds(at, embed), :], preferred_element_type=full).astype(half)
        factors[at_q, at_z, :, rank : 2 * rank] = lax.dot_general(
            (wide * heavy).astype(half), up[:, pl.ds(at, embed)], (((1,), (1,)), ((), ())), preferred_element_type=full
        ).astype(half)
        direct = jnp.sum(wide * (heavy * (1.0 + bias[:, pl.ds(at, embed)])), axis=1, keepdims=True)
        upper = direct.astype(half).astype(full)
        lane = lax.broadcasted_iota(jnp.int32, (row_count * rows, 128), 1)
        both = jnp.where(lane == 0, upper, jnp.where(lane == 1, direct - upper, 0.0))
        factors[at_q, at_z, :, 2 * rank :] = both.astype(half)
        return carry

    lax.fori_loop(0, z_count * q_count, one_table, 0)

    own[q] = mine[:, :, pl.ds(pl.multiple_of(q * samples, 128), samples)]
    total = None
    for at_q in [q] + q_peers:
        if at_q is not q:
            remote(own.at[at_q], own.at[at_q], own_send.at[at_q], own_recv.at[at_q], device(z, at_q, c)).wait_recv()
        term = lax.dot_general(
            own[at_q].reshape(z_count * row_count * rows, samples),
            factors[at_q].reshape(z_count * row_count * rows, 2 * rank + 128),
            (((0,), (0,)), ((), ())), preferred_element_type=full,
        )
        total = term if total is None else total + term
    logits = jnp.sum(total[:, 2 * rank :], axis=1, keepdims=True)
    logits = logits + jnp.sum(total[:, :rank] * total[:, rank : 2 * rank], axis=1, keepdims=True)
    own_row = lax.broadcasted_iota(jnp.int32, (samples, samples), 0)
    own_lane = lax.broadcasted_iota(jnp.int32, (samples, samples), 1)
    clicked = jnp.sum(jnp.where(own_row == own_lane, labels[...].astype(full), 0.0), axis=1, keepdims=True)
    grad = jax.nn.sigmoid(logits) - clicked
    scaled[q, :, : 2 * rank] = (total[:, : 2 * rank] * grad).astype(half)
    lane = lax.broadcasted_iota(jnp.int32, (samples, 128), 1)
    scaled[q, :, 2 * rank :] = jnp.where(lane == 0, grad, 0.0).astype(half)
    spans = (pl.ds(0, rank), pl.ds(rank, rank + 128))
    for turn, span in enumerate(spans):
        for at_q in q_peers:
            sends.append(remote(
                scaled.at[q, :, span], scaled.at[q, :, span],
                scaled_send.at[turn, at_q], scaled_recv.at[turn, q], device(z, at_q, c),
            ))
            sends[-1].start()
    for turn, span in enumerate(spans):
        for at_q in q_peers:
            remote(
                scaled.at[at_q, :, span], scaled.at[at_q, :, span],
                scaled_send.at[turn, at_q], scaled_recv.at[turn, at_q], device(z, at_q, c),
            ).wait_recv()
        gathered = scaled[:, :, span].reshape(q_count * samples, span.size)
        for at_z in z_peers + [z]:
            counted = mine[pl.ds(at_z * row_count, row_count)].reshape(row_count * rows, q_count * samples)
            term = jnp.dot(counted, gathered, preferred_element_type=full).astype(half)
            part_send[pl.ds(at_z * row_count, row_count), :, span] = term.reshape(row_count, rows, span.size)
            for at_c in [c] + c_peers:
                if at_z is z and at_c is c:
                    continue
                to = at_z * row_count + at_c
                sends.append(remote(
                    part_send.at[to, :, span], parts.at[group, :, span],
                    part_send_sem.at[turn, to], part_recv_sem.at[turn, group], device(at_z, q, at_c),
                ))
                sends[-1].start()
    sums = []
    for turn, span in enumerate(spans):
        summed = part_send[group, :, span].astype(full)
        for at_z, at_c in group_peers:
            index = at_z * row_count + at_c
            remote(
                parts.at[index, :, span], parts.at[index, :, span],
                part_send_sem.at[turn, index], part_recv_sem.at[turn, index], device(at_z, q, at_c),
            ).wait_recv()
            summed = summed + parts[index, :, span].astype(full)
        sums.append(summed)
    summed = jnp.concatenate(sums, axis=1)
    whole[c] = summed.astype(half)
    for at_c in c_peers:
        sends.append(remote(whole.at[c], whole.at[c], whole_send.at[at_c], whole_recv.at[c], device(z, q, at_c)))
        sends[-1].start()
    if inside:
        slab_grad, down_grad, up_grad, bias_grad, out_grad = outs
        at = pl.multiple_of((z * q_count + q) * embed, 128)
        heavy, raised = weight[:, pl.ds(at, embed)], 1.0 + bias[:, pl.ds(at, embed)]
        back = jnp.dot(summed[:, :rank].astype(half), up[:, pl.ds(at, embed)], preferred_element_type=full)
        slab_grad[...] = (
            raised * heavy * summed[:, 2 * rank : 2 * rank + 1]
            + heavy * back
            + lax.dot_general(
                summed[:, rank : 2 * rank].astype(half), down[pl.ds(at, embed), :],
                (((1,), (1,)), ((), ())), preferred_element_type=full,
            )
        )
    else:
        sum_out, whole_out, slab_out = outs
        sum_out[...] = summed
        slab_out[...] = slabs[q, z].reshape(row_count * rows, embed)
    for at_c in c_peers:
        remote(whole.at[at_c], whole.at[at_c], whole_send.at[at_c], whole_recv.at[at_c], device(z, q, at_c)).wait_recv()
    everything = whole[...].reshape(row_count * rows, 2 * rank + 128)
    if inside:
        columns = embed // row_count
        place = pl.multiple_of(c * columns, 128)
        mixed = slabs[q, z, :, :, pl.ds(place, columns)].reshape(row_count * rows, columns)
        first = (((0,), (0,)), ((), ()))
        at = pl.multiple_of((z * q_count + q) * embed + c * columns, 128)
        heavy, raised = weight[:, pl.ds(at, columns)], 1.0 + bias[:, pl.ds(at, columns)]
        down_grad[...] = lax.dot_general(mixed, everything[:, rank : 2 * rank], first, preferred_element_type=full).astype(half)
        core = lax.dot_general(everything[:, :rank], mixed, first, preferred_element_type=full)
        up_grad[...] = (core * heavy).astype(half)
        counted = lax.dot_general(everything[:, 2 * rank :], mixed, first, preferred_element_type=full)[:1]
        bias_grad[...] = heavy * counted
        out_grad[...] = raised * counted + jnp.sum(up[:, pl.ds(at, columns)].astype(full) * core, axis=0, keepdims=True)
    else:
        whole_out[...] = everything
    for copy in sends:
        copy.wait_send()
    for at_q in q_peers:
        remote(own.at[at_q], own.at[at_q], own_send.at[at_q], own_recv.at[at_q], device(z, at_q, c)).wait_send()
    for at_c in c_peers:
        remote(slabs.at[:, :, at_c], slabs.at[:, :, at_c], slab_r_send.at[at_c], slab_r_recv.at[at_c], device(z, q, at_c)).wait_send()


def local(slab, counts, cross_down, cross_up, cross_bias, out_weight, labels):
    z_count, q_count, row_count = (lax.axis_size(name) for name in ("z", "q", "row"))
    rows, embed = slab.shape
    samples = labels.shape[0]
    rank, width = cross_down.shape[1], cross_down.shape[0]
    half, full = jnp.bfloat16, jnp.float32
    dot = functools.partial(jnp.einsum, preferred_element_type=full)
    groups, table_rows, wide = z_count * row_count, row_count * rows, 2 * rank + 128
    vmem, anywhere = pl.BlockSpec(memory_space=pltpu.VMEM), pl.BlockSpec(memory_space=pl.ANY)
    sem = pltpu.SemaphoreType.DMA
    columns = embed // row_count
    inside = columns % 128 == 0
    if inside:
        shapes = (
            jax.ShapeDtypeStruct((rows, embed), full),
            jax.ShapeDtypeStruct((columns, rank), half),
            jax.ShapeDtypeStruct((rank, columns), half),
            jax.ShapeDtypeStruct((1, columns), full),
            jax.ShapeDtypeStruct((1, columns), full),
        )
    else:
        shapes = (
            jax.ShapeDtypeStruct((rows, wide), full),
            jax.ShapeDtypeStruct((table_rows, wide), half),
            jax.ShapeDtypeStruct((table_rows, embed), half),
        )
    results = pl.pallas_call(
        functools.partial(kernel, inside, len(shapes)),
        out_shape=shapes,
        in_specs=[vmem, vmem, anywhere, anywhere, vmem, vmem, vmem],
        out_specs=(vmem,) * len(shapes),
        scratch_shapes=[
            pltpu.VMEM((width, rank), half),
            pltpu.VMEM((rank, width), half),
            pltpu.VMEM((groups, rows, q_count * samples), half),
            pltpu.VMEM((groups, rows, q_count * samples), half),
            pltpu.VMEM((q_count, groups, rows, samples), half),
            pltpu.VMEM((q_count, z_count, row_count, rows, embed), half),
            pltpu.VMEM((q_count, z_count, table_rows, wide), half),
            pltpu.VMEM((q_count, samples, wide), half),
            pltpu.VMEM((groups, rows, wide), half),
            pltpu.VMEM((groups, rows, wide), half),
            pltpu.VMEM((row_count, rows, wide), half),
            sem((2,)),
            sem((groups,)), sem((groups,)), sem((q_count,)), sem((q_count,)),
            sem((z_count,)), sem((z_count,)), sem((q_count,)), sem((q_count,)), sem((row_count,)), sem((row_count,)),
            sem((2, q_count)), sem((2, q_count)), sem((2, groups)), sem((2, groups)), sem((row_count,)), sem((row_count,)),
        ],
        compiler_params=pltpu.CompilerParams(collective_id=0, has_side_effects=True, vmem_limit_bytes=60 * 2**20),
    )(slab, counts.T, cross_down, cross_up, cross_bias.reshape(1, -1), out_weight.reshape(1, -1), labels.reshape(1, -1))
    if inside:
        slab_grad, down_grad, up_grad, bias_grad, out_grad = results
        return slab_grad, down_grad, up_grad, bias_grad.reshape(-1), out_grad.reshape(-1)
    summed, whole, slab_table = results
    my_table = lax.axis_index("z") * q_count + lax.axis_index("q")
    start = my_table * embed
    down_own = lax.dynamic_slice_in_dim(cross_down, start, embed, 0)
    up_own = lax.dynamic_slice_in_dim(cross_up, start, embed, 1)
    weight_own = lax.dynamic_slice_in_dim(out_weight, start, embed, 0)
    bias_own = lax.dynamic_slice_in_dim(cross_bias, start, embed, 0)
    left, right, count_sum = summed[:, :rank], summed[:, rank : 2 * rank], summed[:, 2 * rank :][:, :1]
    grad_slab = (
        (1.0 + bias_own) * weight_own * count_sum
        + weight_own * dot("pr,re->pe", left.astype(half), up_own)
        + dot("pr,er->pe", right.astype(half), down_own)
    )
    columns = embed // row_count
    at = lax.axis_index("row") * columns
    slab_own = lax.dynamic_slice_in_dim(slab_table, at, columns, 1)
    weight_part = lax.dynamic_slice_in_dim(weight_own, at, columns, 0)
    bias_part = lax.dynamic_slice_in_dim(bias_own, at, columns, 0)
    up_part = lax.dynamic_slice_in_dim(up_own, at, columns, 1)
    grad_down = dot("pe,pr->er", slab_own, whole[:, rank : 2 * rank])
    core = dot("pr,pe->re", whole[:, :rank], slab_own)
    total = dot("pe,pr->er", slab_own, whole[:, 2 * rank :])[:, 0]
    grad_bias = weight_part * total
    grad_out = (1.0 + bias_part) * total + jnp.sum(up_part.astype(full) * core, axis=0)
    return (
        grad_slab,
        grad_down.astype(half),
        (core * weight_part).astype(half),
        grad_bias,
        grad_out,
    )


def solution(mesh):
    tbl_count, row_count = mesh.shape["tbl"], mesh.shape["row"]
    q_count = inner_count(tbl_count)
    finer = Mesh(mesh.devices.reshape(tbl_count // q_count, q_count, row_count), ("z", "q", "row"))
    every = ("z", "q", "row")
    placed = (P(every, None), P(None, every), P(), P(), P(), P(), P(every))
    return jax.shard_map(
        local,
        mesh=finer,
        in_specs=placed,
        out_specs=(P(every, None), P(every, None), P(None, every), P(every), P(every)),
        check_vma=False,
    )
```

```python
import functools
import math

import jax
import jax.numpy as jnp
from jax import lax
from jax.experimental import pallas as pl
from jax.experimental.pallas import tpu as pltpu
from jax.sharding import Mesh, PartitionSpec as P


def inner_count(count):
    width = max(1, math.isqrt(count))
    while count % width:
        width -= 1
    return width


def kernel(
    inside, out_count, slab, flipped, down_hbm, up_hbm, bias, weight, labels,
    *refs,
):
    outs, rest = refs[:out_count], refs[out_count:]
    (
    down, up, send_counts, mine, own, slabs, factors, scaled, part_send, parts, whole,
    load_sem, count_send, count_recv, own_send, own_recv,
    slab_z_send, slab_z_recv, slab_q_send, slab_q_recv, slab_r_send, slab_r_recv,
    scaled_send, scaled_recv, part_send_sem, part_recv_sem, whole_send, whole_recv,
    ) = rest
    z_count, q_count, row_count = (lax.axis_size(name) for name in ("z", "q", "row"))
    z, q, c = (lax.axis_index(name) for name in ("z", "q", "row"))
    rows, embed = slab.shape
    samples = labels.shape[1]
    rank = down.shape[1]
    half, full = jnp.bfloat16, jnp.float32
    group = z * row_count + c

    def device(at_z, at_q, at_c):
        return (at_z, at_q, at_c)

    def remote(source, target, send, recv, to):
        return pltpu.make_async_remote_copy(
            src_ref=source, dst_ref=target, send_sem=send, recv_sem=recv,
            device_id=to, device_id_type=pl.DeviceIdType.MESH,
        )

    z_peers = [lax.rem(z + step, z_count) for step in range(1, z_count)]
    q_peers = [lax.rem(q + step, q_count) for step in range(1, q_count)]
    c_peers = [lax.rem(c + step, row_count) for step in range(1, row_count)]
    group_peers = [(z, at_c) for at_c in c_peers]
    for at_z in z_peers:
        group_peers += [(at_z, at_c) for at_c in [c] + c_peers]

    loads = [
        pltpu.make_async_copy(down_hbm, down, load_sem.at[0]),
        pltpu.make_async_copy(up_hbm, up, load_sem.at[1]),
    ]
    for load in loads:
        load.start()
    barrier = pltpu.get_barrier_semaphore()
    for at_z, at_c in group_peers:
        pl.semaphore_signal(barrier, inc=1, device_id=device(at_z, q, at_c), device_id_type=pl.DeviceIdType.MESH)
    for at_q in q_peers:
        pl.semaphore_signal(barrier, inc=1, device_id=device(z, at_q, c), device_id_type=pl.DeviceIdType.MESH)
    slabs[q, z, c] = slab[...]

    def fill(at_z, at_c):
        for at_q in range(q_count):
            start = pl.multiple_of(((at_z * q_count + at_q) * row_count + at_c) * samples, 128)
            block = flipped[:, pl.ds(start, samples)].astype(half)
            if at_z is z and at_c is c:
                mine[group, :, at_q * samples : (at_q + 1) * samples] = block
            else:
                send_counts[at_z * row_count + at_c, :, at_q * samples : (at_q + 1) * samples] = block

    for at_z, at_c in group_peers:
        fill(at_z, at_c)
    pl.semaphore_wait(barrier, len(group_peers) + len(q_peers))

    sends = []
    for at_z in z_peers:
        sends.append(remote(slabs.at[q, z, c], slabs.at[q, z, c], slab_z_send.at[at_z], slab_z_recv.at[z], device(at_z, q, c)))
        sends[-1].start()
    for at_z, at_c in group_peers:
        to = at_z * row_count + at_c
        sends.append(remote(send_counts.at[to], mine.at[group], count_send.at[to], count_recv.at[group], device(at_z, q, at_c)))
        sends[-1].start()
    fill(z, c)

    def forward_counts(index):
        for at_q in q_peers:
            block = mine.at[index, :, pl.ds(pl.multiple_of(at_q * samples, 128), samples)]
            remote(block, own.at[q, index], own_send.at[at_q], own_recv.at[q], device(z, at_q, c)).start()

    def receive_counts(peers):
        for at_z, at_c in peers:
            index = at_z * row_count + at_c
            remote(mine.at[index], mine.at[index], count_send.at[index], count_recv.at[index], device(at_z, q, at_c)).wait_recv()
            forward_counts(index)

    forward_counts(group)
    receive_counts(group_peers[: row_count - 1])
    for at_z in z_peers:
        remote(slabs.at[q, at_z, c], slabs.at[q, at_z, c], slab_z_send.at[at_z], slab_z_recv.at[at_z], device(at_z, q, c)).wait_recv()
    for at_q in q_peers:
        sends.append(remote(slabs.at[q, :, c], slabs.at[q, :, c], slab_q_send.at[at_q], slab_q_recv.at[q], device(z, at_q, c)))
        sends[-1].start()
    for at_c in c_peers:
        remote(slabs.at[q, :, c], slabs.at[q, :, c], slab_r_send.at[at_c], slab_r_recv.at[c], device(z, q, at_c)).start()
    for at_q in q_peers:
        remote(slabs.at[at_q, :, c], slabs.at[at_q, :, c], slab_q_send.at[at_q], slab_q_recv.at[at_q], device(z, at_q, c)).wait_recv()
        for at_c in c_peers:
            remote(slabs.at[at_q, :, c], slabs.at[at_q, :, c], slab_r_send.at[at_c], slab_r_recv.at[c], device(z, q, at_c)).start()

    receive_counts(group_peers[row_count - 1 :])
    for at_c in c_peers:
        remote(slabs.at[:, :, at_c], slabs.at[:, :, at_c], slab_r_send.at[at_c], slab_r_recv.at[at_c], device(z, q, at_c)).wait_recv()

    for load in loads:
        load.wait()

    def one_table(table, carry):
        at = pl.multiple_of(table * embed, 128)
        at_z, at_q = table // q_count, lax.rem(table, q_count)
        block = slabs[at_q, at_z].reshape(row_count * rows, embed)
        wide = block.astype(full)
        heavy = weight[:, pl.ds(at, embed)]
        factors[at_q, at_z, :, :rank] = jnp.dot(block, down[pl.ds(at, embed), :], preferred_element_type=full).astype(half)
        factors[at_q, at_z, :, rank : 2 * rank] = lax.dot_general(
            (wide * heavy).astype(half), up[:, pl.ds(at, embed)], (((1,), (1,)), ((), ())), preferred_element_type=full
        ).astype(half)
        direct = jnp.sum(wide * (heavy * (1.0 + bias[:, pl.ds(at, embed)])), axis=1, keepdims=True)
        upper = direct.astype(half).astype(full)
        lane = lax.broadcasted_iota(jnp.int32, (row_count * rows, 128), 1)
        both = jnp.where(lane == 0, upper, jnp.where(lane == 1, direct - upper, 0.0))
        factors[at_q, at_z, :, 2 * rank :] = both.astype(half)
        return carry

    lax.fori_loop(0, z_count * q_count, one_table, 0)

    own[q] = mine[:, :, pl.ds(pl.multiple_of(q * samples, 128), samples)]
    total = None
    for at_q in [q] + q_peers:
        if at_q is not q:
            remote(own.at[at_q], own.at[at_q], own_send.at[at_q], own_recv.at[at_q], device(z, at_q, c)).wait_recv()
        term = lax.dot_general(
            own[at_q].reshape(z_count * row_count * rows, samples),
            factors[at_q].reshape(z_count * row_count * rows, 2 * rank + 128),
            (((0,), (0,)), ((), ())), preferred_element_type=full,
        )
        total = term if total is None else total + term
    logits = jnp.sum(total[:, 2 * rank :], axis=1, keepdims=True)
    logits = logits + jnp.sum(total[:, :rank] * total[:, rank : 2 * rank], axis=1, keepdims=True)
    own_row = lax.broadcasted_iota(jnp.int32, (samples, samples), 0)
    own_lane = lax.broadcasted_iota(jnp.int32, (samples, samples), 1)
    clicked = jnp.sum(jnp.where(own_row == own_lane, labels[...].astype(full), 0.0), axis=1, keepdims=True)
    grad = jax.nn.sigmoid(logits) - clicked
    scaled[q, :, : 2 * rank] = (total[:, : 2 * rank] * grad).astype(half)
    lane = lax.broadcasted_iota(jnp.int32, (samples, 128), 1)
    scaled[q, :, 2 * rank :] = jnp.where(lane == 0, grad, 0.0).astype(half)
    spans = (pl.ds(0, rank), pl.ds(rank, rank + 128))
    for turn, span in enumerate(spans):
        for at_q in q_peers:
            sends.append(remote(
                scaled.at[q, :, span], scaled.at[q, :, span],
                scaled_send.at[turn, at_q], scaled_recv.at[turn, q], device(z, at_q, c),
            ))
            sends[-1].start()
    for turn, span in enumerate(spans):
        for at_q in q_peers:
            remote(
                scaled.at[at_q, :, span], scaled.at[at_q, :, span],
                scaled_send.at[turn, at_q], scaled_recv.at[turn, at_q], device(z, at_q, c),
            ).wait_recv()
        gathered = scaled[:, :, span].reshape(q_count * samples, span.size)
        for at_z in z_peers + [z]:
            counted = mine[pl.ds(at_z * row_count, row_count)].reshape(row_count * rows, q_count * samples)
            term = jnp.dot(counted, gathered, preferred_element_type=full).astype(half)
            part_send[pl.ds(at_z * row_count, row_count), :, span] = term.reshape(row_count, rows, span.size)
            for at_c in [c] + c_peers:
                if at_z is z and at_c is c:
                    continue
                to = at_z * row_count + at_c
                sends.append(remote(
                    part_send.at[to, :, span], parts.at[group, :, span],
                    part_send_sem.at[turn, to], part_recv_sem.at[turn, group], device(at_z, q, at_c),
                ))
                sends[-1].start()
    sums = []
    for turn, span in enumerate(spans):
        summed = part_send[group, :, span].astype(full)
        for at_z, at_c in group_peers:
            index = at_z * row_count + at_c
            remote(
                parts.at[index, :, span], parts.at[index, :, span],
                part_send_sem.at[turn, index], part_recv_sem.at[turn, index], device(at_z, q, at_c),
            ).wait_recv()
            summed = summed + parts[index, :, span].astype(full)
        sums.append(summed)
    summed = jnp.concatenate(sums, axis=1)
    whole[c] = summed.astype(half)
    for at_c in c_peers:
        sends.append(remote(whole.at[c], whole.at[c], whole_send.at[at_c], whole_recv.at[c], device(z, q, at_c)))
        sends[-1].start()
    if inside:
        slab_grad, down_grad, up_grad, bias_grad, out_grad = outs
        at = pl.multiple_of((z * q_count + q) * embed, 128)
        heavy, raised = weight[:, pl.ds(at, embed)], 1.0 + bias[:, pl.ds(at, embed)]
        back = jnp.dot(summed[:, :rank].astype(half), up[:, pl.ds(at, embed)], preferred_element_type=full)
        slab_grad[...] = (
            raised * heavy * summed[:, 2 * rank : 2 * rank + 1]
            + heavy * back
            + lax.dot_general(
                summed[:, rank : 2 * rank].astype(half), down[pl.ds(at, embed), :],
                (((1,), (1,)), ((), ())), preferred_element_type=full,
            )
        )
    else:
        sum_out, whole_out, slab_out = outs
        sum_out[...] = summed
        slab_out[...] = slabs[q, z].reshape(row_count * rows, embed)
    for at_c in c_peers:
        remote(whole.at[at_c], whole.at[at_c], whole_send.at[at_c], whole_recv.at[at_c], device(z, q, at_c)).wait_recv()
    everything = whole[...].reshape(row_count * rows, 2 * rank + 128)
    if inside:
        columns = embed // row_count
        place = pl.multiple_of(c * columns, 128)
        mixed = slabs[q, z, :, :, pl.ds(place, columns)].reshape(row_count * rows, columns)
        first = (((0,), (0,)), ((), ()))
        at = pl.multiple_of((z * q_count + q) * embed + c * columns, 128)
        heavy, raised = weight[:, pl.ds(at, columns)], 1.0 + bias[:, pl.ds(at, columns)]
        down_grad[...] = lax.dot_general(mixed, everything[:, rank : 2 * rank], first, preferred_element_type=full).astype(half)
        core = lax.dot_general(everything[:, :rank], mixed, first, preferred_element_type=full)
        up_grad[...] = (core * heavy).astype(half)
        counted = lax.dot_general(everything[:, 2 * rank :], mixed, first, preferred_element_type=full)[:1]
        bias_grad[...] = heavy * counted
        out_grad[...] = raised * counted + jnp.sum(up[:, pl.ds(at, columns)].astype(full) * core, axis=0, keepdims=True)
    else:
        whole_out[...] = everything
    for copy in sends:
        copy.wait_send()
    for at_q in q_peers:
        remote(own.at[at_q], own.at[at_q], own_send.at[at_q], own_recv.at[at_q], device(z, at_q, c)).wait_send()
    for at_c in c_peers:
        remote(slabs.at[:, :, at_c], slabs.at[:, :, at_c], slab_r_send.at[at_c], slab_r_recv.at[at_c], device(z, q, at_c)).wait_send()


def local(slab, counts, cross_down, cross_up, cross_bias, out_weight, labels):
    z_count, q_count, row_count = (lax.axis_size(name) for name in ("z", "q", "row"))
    rows, embed = slab.shape
    samples = labels.shape[0]
    rank, width = cross_down.shape[1], cross_down.shape[0]
    half, full = jnp.bfloat16, jnp.float32
    dot = functools.partial(jnp.einsum, preferred_element_type=full)
    groups, table_rows, wide = z_count * row_count, row_count * rows, 2 * rank + 128
    vmem, anywhere = pl.BlockSpec(memory_space=pltpu.VMEM), pl.BlockSpec(memory_space=pl.ANY)
    sem = pltpu.SemaphoreType.DMA
    columns = embed // row_count
    inside = columns % 128 == 0
    if inside:
        shapes = (
            jax.ShapeDtypeStruct((rows, embed), full),
            jax.ShapeDtypeStruct((columns, rank), half),
            jax.ShapeDtypeStruct((rank, columns), half),
            jax.ShapeDtypeStruct((1, columns), full),
            jax.ShapeDtypeStruct((1, columns), full),
        )
    else:
        shapes = (
            jax.ShapeDtypeStruct((rows, wide), full),
            jax.ShapeDtypeStruct((table_rows, wide), half),
            jax.ShapeDtypeStruct((table_rows, embed), half),
        )
    results = pl.pallas_call(
        functools.partial(kernel, inside, len(shapes)),
        out_shape=shapes,
        in_specs=[vmem, vmem, anywhere, anywhere, vmem, vmem, vmem],
        out_specs=(vmem,) * len(shapes),
        scratch_shapes=[
            pltpu.VMEM((width, rank), half),
            pltpu.VMEM((rank, width), half),
            pltpu.VMEM((groups, rows, q_count * samples), half),
            pltpu.VMEM((groups, rows, q_count * samples), half),
            pltpu.VMEM((q_count, groups, rows, samples), half),
            pltpu.VMEM((q_count, z_count, row_count, rows, embed), half),
            pltpu.VMEM((q_count, z_count, table_rows, wide), half),
            pltpu.VMEM((q_count, samples, wide), half),
            pltpu.VMEM((groups, rows, wide), half),
            pltpu.VMEM((groups, rows, wide), half),
            pltpu.VMEM((row_count, rows, wide), half),
            sem((2,)),
            sem((groups,)), sem((groups,)), sem((q_count,)), sem((q_count,)),
            sem((z_count,)), sem((z_count,)), sem((q_count,)), sem((q_count,)), sem((row_count,)), sem((row_count,)),
            sem((2, q_count)), sem((2, q_count)), sem((2, groups)), sem((2, groups)), sem((row_count,)), sem((row_count,)),
        ],
        compiler_params=pltpu.CompilerParams(collective_id=0, has_side_effects=True, vmem_limit_bytes=60 * 2**20),
    )(slab, counts.T, cross_down, cross_up, cross_bias.reshape(1, -1), out_weight.reshape(1, -1), labels.reshape(1, -1))
    if inside:
        slab_grad, down_grad, up_grad, bias_grad, out_grad = results
        return slab_grad, down_grad, up_grad, bias_grad.reshape(-1), out_grad.reshape(-1)
    summed, whole, slab_table = results
    my_table = lax.axis_index("z") * q_count + lax.axis_index("q")
    start = my_table * embed
    down_own = lax.dynamic_slice_in_dim(cross_down, start, embed, 0)
    up_own = lax.dynamic_slice_in_dim(cross_up, start, embed, 1)
    weight_own = lax.dynamic_slice_in_dim(out_weight, start, embed, 0)
    bias_own = lax.dynamic_slice_in_dim(cross_bias, start, embed, 0)
    left, right, count_sum = summed[:, :rank], summed[:, rank : 2 * rank], summed[:, 2 * rank :][:, :1]
    grad_slab = (
        (1.0 + bias_own) * weight_own * count_sum
        + weight_own * dot("pr,re->pe", left.astype(half), up_own)
        + dot("pr,er->pe", right.astype(half), down_own)
    )
    columns = embed // row_count
    at = lax.axis_index("row") * columns
    slab_own = lax.dynamic_slice_in_dim(slab_table, at, columns, 1)
    weight_part = lax.dynamic_slice_in_dim(weight_own, at, columns, 0)
    bias_part = lax.dynamic_slice_in_dim(bias_own, at, columns, 0)
    up_part = lax.dynamic_slice_in_dim(up_own, at, columns, 1)
    grad_down = dot("pe,pr->er", slab_own, whole[:, rank : 2 * rank])
    core = dot("pr,pe->re", whole[:, :rank], slab_own)
    total = dot("pe,pr->er", slab_own, whole[:, 2 * rank :])[:, 0]
    grad_bias = weight_part * total
    grad_out = (1.0 + bias_part) * total + jnp.sum(up_part.astype(full) * core, axis=0)
    return (
        grad_slab,
        grad_down.astype(half),
        (core * weight_part).astype(half),
        grad_bias,
        grad_out,
    )


def solution(mesh):
    tbl_count, row_count = mesh.shape["tbl"], mesh.shape["row"]
    q_count = inner_count(tbl_count)
    finer = Mesh(mesh.devices.reshape(tbl_count // q_count, q_count, row_count), ("z", "q", "row"))
    every = ("z", "q", "row")
    placed = (P(every, None), P(None, every), P(), P(), P(), P(), P(every))
    return jax.shard_map(
        local,
        mesh=finer,
        in_specs=placed,
        out_specs=(P(every, None), P(every, None), P(None, every), P(every), P(every)),
        check_vma=False,
    )
```
